128 devices in a mesh: trip: 8 (over x, core), exc: 16 (over y, z).
Axes of the slice: x: 4, y: 4, z: 4, core: 2. Of those that a mesh axis runs over, the one named last changes fastest.
Arguments:
- pes_grids: float32 [512, 16, 256], P(('trip', 'exc')), may hold values from -6 to 6
- modals: float32 [200, 128], P('trip'), may hold values from -1.8 to 1.8
- energies: float32 [200, 8], P('trip'), may hold values from 0.05 to 0.5
- triple_modes: int32 [512, 3], P(('trip', 'exc')), may hold values from 0 to 199, as said below
- routing: int32 [8, 16, 16], P('trip', None, 'exc'), may hold values from 0 to 3
- block_source: int32 [3072], P(('trip', 'exc')), may hold values from 0 to 15
- live_rows: int32 [3072], P(('trip', 'exc')), may hold values from 1 to 8
- trial_vectors: bfloat16 [3072, 512, 512], P(('trip', 'exc')), may hold values from -6 to 6
- spectator_energy: float32 [3072, 8], P(('trip', 'exc')), may hold values from 0.1 to 1
Outputs:
- sigma_blocks: bfloat16 [3072, 512, 512], P(('trip', 'exc'))
The draws below stay inside these ranges and needn't reach their ends.
Inputs may be any that keep to these rules, and one draw needn't show every extreme that they name: `triple_modes`: the three modes of a triple are distinct.
All inputs are finite; a program needn't handle non-finite values.
Results may differ from the reference program's by a relative error of at most 0.005.
Values may be sent and summed in bfloat16 or wider, within the bound.
No kernel may reach another device: no remote copies, remote signals or barrier semaphores. Data moves between devices by JAX's collectives and lax.ppermute only.
A program may use at most 128 MiB of HBM per device.

```python
import math
import jax
import jax.numpy as jnp
import numpy as np
from jax import lax

MODES = 200
NMOD = 8
G = 16
NVEC = 64
ROWS = 8
BLK_DEV = 24
TRI_DEV = 4
S = 512
SLABS = 8
COLS = 16
NTRI = 512
NBLK = 3072


def draw_triple_modes(key, part):
    subkeys = jax.random.split(key, 3)
    mode_one = jax.random.randint(subkeys[0], (NTRI,), 0, MODES)
    step_one = jax.random.randint(subkeys[1], (NTRI,), 1, MODES // 2)
    step_two = jax.random.randint(subkeys[2], (NTRI,), 1, MODES // 2)
    mode_two = (mode_one + step_one) % MODES
    mode_three = (mode_two + step_two) % MODES
    return jnp.stack([mode_one, mode_two, mode_three], axis=1).astype(jnp.int32)


def draw_live_rows(key, part):
    subkeys = jax.random.split(key, 2)
    drawn = jax.random.randint(subkeys[0], (NBLK,), 1, ROWS + 1)
    chosen = jax.random.randint(subkeys[1], (), 0, NBLK)
    return drawn.at[chosen].set(ROWS).astype(jnp.int32)


def with_ends(entries, own_key, smallest, largest):
    spot = [jax.random.randint(jax.random.fold_in(own_key, axis), (), 0, length) for axis, length in enumerate(entries.shape)]
    main_axis = entries.shape.index(max(entries.shape))
    beside = spot[:main_axis] + [(spot[main_axis] + 1) % entries.shape[main_axis]] + spot[main_axis + 1:]
    return entries.at[tuple(spot)].set(smallest).at[tuple(beside)].set(largest)


def steps_of(key, extent, cuts, smallest, largest):
    gain, own = 1.0, jax.random.fold_in(key, 6)
    for position, shards_of in cuts:
        heights = jnp.exp(jax.random.uniform(jax.random.fold_in(own, position), (shards_of,), jnp.float32, smallest / len(cuts), largest / len(cuts)))
        gain = gain * jnp.repeat(heights, extent[position] // shards_of).reshape([-1 if axis == position else 1 for axis in range(len(extent))])
    return gain


def rank_bounds(number_of, slope):
    portions = [(1 << 20) // math.isqrt(grade ** slope) + 1 for grade in range(1, number_of + 1)]
    width = 1 + sum(portions) // (1 << 30)
    return np.cumsum(np.array([max(1, weight // width) for weight in portions]))


def ranked(own_key, dims, count, lean):
    grid = rank_bounds(count, lean)
    lot = jax.random.randint(jax.random.fold_in(own_key, 1), dims, 0, int(grid[count - 1]))
    grade = jnp.searchsorted(jnp.asarray(grid, jnp.int32), lot, side="right")
    return jax.random.permutation(jax.random.fold_in(own_key, 2), count)[grade].astype(jnp.int32)


def normal_values(rng, dims, scale, most, pieces=(), kind=jnp.bfloat16):
    result = jax.random.normal(rng, dims, jnp.float32) * scale
    if len(pieces) > 0:
        result = steps_of(rng, dims, pieces, -0.22, 0.18) * result
    return jnp.clip(result, min=-most, max=most).astype(kind)


def setup_inputs(seed: int = 0) -> dict:
    key_of = jax.random.split(jax.random.key(seed), 10)
    pes_grids = normal_values(key_of[0], (NTRI, G, G * G), 1.0, 6.0, ((0, 128),), jnp.float32)
    modals = normal_values(key_of[1], (MODES, NMOD * G), 0.3, 1.8, ((0, 8),), jnp.float32)
    energies = jnp.clip(jnp.exp(math.log(0.5) - 2.3025851 * jax.random.uniform(key_of[2], (MODES, NMOD), jnp.float32) ** steps_of(key_of[2], (MODES, NMOD), ((0, 8),), -0.2, 0.2)), 0.05, 0.5)
    triple_modes = draw_triple_modes(jax.random.fold_in(key_of[9], 71), 0)
    routing = with_ends(jax.random.randint(key_of[4], (SLABS, COLS, COLS), 0, TRI_DEV), jax.random.fold_in(key_of[4], 1), 0, TRI_DEV - 1).astype(jnp.int32)
    block_source = with_ends(ranked(key_of[5], (NBLK,), COLS, 2), jax.random.fold_in(key_of[5], 3), 0, COLS - 1).astype(jnp.int32)
    live_rows = draw_live_rows(jax.random.fold_in(key_of[9], 71), 0)
    trial_vectors = normal_values(key_of[7], (NBLK, S, ROWS * NVEC), 1.0, 6.0, ((0, 128),))
    spectator_energy = jnp.clip(jnp.exp(math.log(1.0) - 2.3025851 * jax.random.uniform(key_of[8], (NBLK, ROWS), jnp.float32) ** steps_of(key_of[8], (NBLK, ROWS), ((0, 128),), -0.2, 0.2)), 0.1, 1.0)
    return dict(pes_grids=pes_grids, modals=modals, energies=energies, triple_modes=triple_modes, routing=routing, block_source=block_source, live_rows=live_rows, trial_vectors=trial_vectors, spectator_energy=spectator_energy)


def integrals(grid_values, modal_rows, level_rows):
    shaped = modal_rows.reshape(3, NMOD, G)
    paired = (shaped[:, :, None, :] * shaped[:, None, :, :]).reshape(3, NMOD * NMOD, G)
    grid_cube = grid_values.reshape(G, G, G)
    section_one = jnp.einsum("xyz,cz->xyc", grid_cube, paired[2], precision=lax.Precision.HIGHEST)
    section_two = jnp.einsum("xyc,by->xbc", section_one, paired[1], precision=lax.Precision.HIGHEST)
    tensor = jnp.einsum("xbc,ax->abc", section_two, paired[0], precision=lax.Precision.HIGHEST)
    states = NMOD * NMOD * NMOD
    matrix = tensor.reshape(NMOD, NMOD, NMOD, NMOD, NMOD, NMOD).transpose(0, 2, 4, 1, 3, 5).reshape(states, states)
    diagonal = (level_rows[0][:, None, None] + level_rows[1][None, :, None] + level_rows[2][None, None, :]).reshape(states)
    return (matrix + jnp.diag(diagonal)).astype(jnp.bfloat16)


def apply_block(matrix, coeff_block, spec_row, live_count):
    product = jnp.dot(matrix, coeff_block, preferred_element_type=jnp.float32)
    spread = jnp.repeat(spec_row, NVEC)
    summed = product + spread[None, :] * coeff_block.astype(jnp.float32)
    column_rows = jnp.arange(ROWS * NVEC, dtype=jnp.int32) // NVEC
    return jnp.where((column_rows < live_count)[None, :], summed, 0.0).astype(jnp.bfloat16)


def reference(pes_grids, modals, energies, triple_modes, routing, block_source, live_rows, trial_vectors, spectator_energy):
    block_ids = jnp.arange(NBLK, dtype=jnp.int32)
    device = block_ids // BLK_DEV
    slab_of = device // COLS
    column = device % COLS
    local_id = routing[slab_of, column, block_source]
    triple_ids = ((slab_of * COLS + block_source) * TRI_DEV + local_id).astype(jnp.int32)

    def one_block(packed):
        triple_id, coeff_block, spec_row, live_count = packed
        mode_ids = triple_modes[triple_id]
        matrix = integrals(pes_grids[triple_id], modals[mode_ids], energies[mode_ids])
        return apply_block(matrix, coeff_block, spec_row, live_count)

    return lax.map(one_block, (triple_ids, trial_vectors, spectator_energy, live_rows))
```

```python
import jax
import jax.numpy as jnp
from jax import lax
from jax.experimental import pallas as pl
from jax.experimental.pallas import tpu as pltpu
from jax.sharding import PartitionSpec as P

NMOD = 8
G = 16
NVEC = 64
S = 512
HALF = 256
COLS = 16
TRIPS = 8
TABLE_ROWS = 32
PAY_ROWS = 24
XOR_STEPS = (1, 2, 6)
F32 = jnp.float32
BF16 = jnp.bfloat16


def iota(shape, axis):
    return lax.broadcasted_iota(jnp.int32, shape, axis)


def pack_kernel(routing, triple_modes, pes, modals, energies, pay, table):
    lane = iota((8, HALF), 1)
    for q in range(COLS):
        local = routing[0, q, 0]
        pay[q, 0:G, :] = pes[local]
        first = triple_modes[local, 0].astype(F32)
        second = triple_modes[local, 1].astype(F32)
        third = triple_modes[local, 2].astype(F32)
        pay[q, G:PAY_ROWS, :] = jnp.where(lane == 0, first, jnp.where(lane == 1, second, third))
    rows = modals.shape[0]
    table[...] = jnp.zeros_like(table)
    table[0:rows, 0:128] = modals[...]
    table[0:rows, 128 : 128 + NMOD] = energies[...]


def split(x):
    high = x.astype(BF16)
    return high, (x - high.astype(F32)).astype(BF16)


def pick(values, chosen):
    high, low = split(values)
    return jnp.dot(high, chosen, preferred_element_type=F32) + jnp.dot(
        low, chosen, preferred_element_type=F32
    )


def ones_where(condition):
    return jnp.where(condition, 1.0, 0.0).astype(BF16)


def repeat_rows(x, count):
    rows, lanes = x.shape
    return jnp.broadcast_to(x[:, None, :], (rows, count, lanes)).reshape(rows * count, lanes)


def sigma_kernel(
    sources, live, pay, table, spectator, vectors, out,
    held, matrix, zeros, modal_i, modal_j, modal_k, modal_f, level, spread, used, in_sem, out_sem,
):
    blocks = held.shape[0]
    left, right = pl.ds(0, HALF), pl.ds(HALF, HALF)

    def load(b, half, n):
        return pltpu.make_async_copy(vectors.at[b, :, half], held.at[b, :, half], in_sem.at[b, n])

    def store(b, half, n):
        return pltpu.make_async_copy(held.at[b, :, half], out.at[b, :, half], out_sem.at[b, n])

    def blank(b):
        return pltpu.make_async_copy(zeros, out.at[b, :, right], out_sem.at[b, 1])

    zeros[...] = jnp.zeros_like(zeros)
    for s in range(COLS):
        used[s] = 0

    @pl.loop(0, blocks)
    def _(b):
        used[sources[b]] = 1
        load(b, left, 0).start()

        @pl.when(live[b] > 4)
        def _():
            load(b, right, 1).start()

    @pl.loop(0, blocks)
    def _(b):
        @pl.when(live[b] <= 4)
        def _():
            blank(b).start()

    me = lax.axis_index("trip")
    slot, within = iota((1, HALF), 1) // TABLE_ROWS, iota((1, HALF), 1) % TABLE_ROWS
    owner = me ^ (slot & 1) ^ ((slot & 2)) ^ jnp.where((slot & 4) > 0, 6, 0)
    per = 25
    ids = jnp.where(within < per, owner * per + within, -1).astype(F32)
    named = pay[:, G, :]
    chosen = jnp.concatenate([ones_where(named[:, n : n + 1] == ids) for n in range(3)], axis=0)
    high, low = split(table[...])
    rows = jnp.dot(chosen, high, preferred_element_type=F32) + jnp.dot(
        chosen, low, preferred_element_type=F32
    )
    own_modal = iota((128, 128), 1) // G == iota((128, 128), 0) % NMOD
    first, second, third = (
        jnp.where(own_modal, repeat_rows(rows[16 * n : 16 * n + 16, 0:128], NMOD), 0.0)
        for n in range(3)
    )
    by_major = ones_where(iota((128, HALF), 1) // G == iota((128, HALF), 0) % G)
    by_minor = ones_where(iota((128, HALF), 1) % G == iota((128, HALF), 0) % G)
    modal_i[...] = pick(first, by_major)
    modal_j[...] = pick(second, by_major)
    modal_k[...] = pick(third, by_minor)
    own_point = iota((HALF, 128), 1) % G == iota((HALF, 128), 0) % G
    points = jnp.where(own_point, repeat_rows(rows[0:16, 0:128], G), 0.0)
    modal_f[...] = pick(points, ones_where(iota((128, S), 0) // G == iota((128, S), 1) // NVEC))
    row, col = iota((128, S), 0), iota((128, S), 1)
    level[...] = (
        pick(rows[0:16, 128:256], ones_where(row == col // 64))
        + pick(rows[16:32, 128:256], ones_where(row == (col // 8) % 8))
        + pick(rows[32:48, 128:256], ones_where(row == col % 8))
    )
    padded = jnp.concatenate([spectator[...], jnp.zeros((blocks, 120), F32)], axis=1)
    spread[...] = pick(padded, ones_where(row == col // NVEC))

    same = iota((128, HALF), 0) % G == iota((128, HALF), 1) % G

    @pl.loop(0, COLS)
    def _(s):
        @pl.when(used[s] > 0)
        def _():
            eight = pl.ds(pl.multiple_of(s * 8, 8), 8)
            sixteen = pl.ds(pl.multiple_of(s * 16, 16), 16)
            grid = pay[s, 0:G, :]
            pairs = (modal_j[eight, :][:, None, :] * modal_k[eight, :][None, :, :]).reshape(64, HALF)
            high, low = split(pairs)
            weights = jnp.concatenate([high, high, low, low], axis=0)
            mix = jnp.where(same, repeat_rows(modal_i[eight, :], G), 0.0).astype(BF16)
            factor = modal_f[sixteen, :]
            levels = level[pl.ds(s, 1), :]
            for r in range(4):
                part = pairs[16 * r : 16 * r + 16]
                scaled = (grid[:, None, :] * part[None, :, :]).reshape(HALF, HALF).astype(BF16)
                both = lax.dot_general(
                    scaled, weights, (((1,), (1,)), ((), ())), preferred_element_type=F32
                )
                inner = (both[:, 0:128] + both[:, 128:256]).reshape(G, G, 128)
                wide = jnp.concatenate(
                    [
                        (inner * factor[:, None, 128 * j : 128 * j + 128])
                        .reshape(HALF, 128)
                        .astype(BF16)
                        for j in range(4)
                    ],
                    axis=1,
                )
                block = jnp.dot(mix, wide, preferred_element_type=F32)
                for a in range(NMOD):
                    tile = slice(128 * (a // 2), 128 * (a // 2) + 128)
                    at = iota((G, 128), 1) == iota((G, 128), 0) + (64 * (a % 2) + 16 * r)
                    mine = block[16 * a : 16 * a + 16, :]
                    target = slice(64 * a + 16 * r, 64 * a + 16 * r + 16)
                    matrix[s, target, :] = mine.astype(BF16)
                    matrix[s, target, tile] = (
                        mine[:, tile] + jnp.where(at, levels[:, tile], 0.0)
                    ).astype(BF16)

    def apply(b, lanes):
        coeff = held[b, :, 0:lanes]
        product = jnp.dot(matrix[sources[b]], coeff, preferred_element_type=F32)
        summed = product + spread[pl.ds(b, 1), 0:lanes] * coeff.astype(F32)
        kept = iota((1, lanes), 1) < live[b] * NVEC
        held[b, :, 0:lanes] = jnp.where(kept, summed, 0.0).astype(BF16)

    @pl.loop(0, blocks)
    def _(b):
        load(b, left, 0).wait()

        @pl.when(live[b] > 4)
        def _():
            load(b, right, 1).wait()
            apply(b, S)
            store(b, right, 1).start()

        @pl.when(live[b] <= 4)
        def _():
            apply(b, HALF)

        store(b, left, 0).start()

    @pl.loop(0, blocks)
    def _(b):
        store(b, left, 0).wait()
        store(b, right, 1).wait()


def late_call(sources, live, received, table, spectator, vectors):
    vmem, smem = pl.BlockSpec(memory_space=pltpu.VMEM), pl.BlockSpec(memory_space=pltpu.SMEM)
    anywhere = pl.BlockSpec(memory_space=pl.ANY)
    blocks = vectors.shape[0]
    return pl.pallas_call(
        sigma_kernel,
        out_shape=jax.ShapeDtypeStruct(vectors.shape, BF16),
        in_specs=[smem, smem, vmem, vmem, vmem, anywhere],
        out_specs=anywhere,
        scratch_shapes=[
            pltpu.VMEM((blocks, S, S), BF16),
            pltpu.VMEM((COLS, S, S), BF16),
            pltpu.VMEM((S, HALF), BF16),
            pltpu.VMEM((128, HALF), F32),
            pltpu.VMEM((128, HALF), F32),
            pltpu.VMEM((128, HALF), F32),
            pltpu.VMEM((HALF, S), F32),
            pltpu.VMEM((COLS, S), F32),
            pltpu.VMEM((blocks, S), F32),
            pltpu.SMEM((COLS,), jnp.int32),
            pltpu.SemaphoreType.DMA((blocks, 2)),
            pltpu.SemaphoreType.DMA((blocks, 2)),
        ],
        compiler_params=pltpu.CompilerParams(vmem_limit_bytes=48 * 2**20),
        cost_estimate=pl.CostEstimate(
            flops=2 * (blocks + COLS) * S**3, bytes_accessed=4 * blocks * S * S, transcendentals=0
        ),
    )(sources, live, received, table, spectator, vectors)


def on_device(
    pes_grids,
    modals,
    energies,
    triple_modes,
    routing,
    block_source,
    live_rows,
    trial_vectors,
    spectator_energy,
):
    vmem, smem = pl.BlockSpec(memory_space=pltpu.VMEM), pl.BlockSpec(memory_space=pltpu.SMEM)
    pay, table = pl.pallas_call(
        pack_kernel,
        out_shape=(
            jax.ShapeDtypeStruct((COLS, PAY_ROWS, HALF), F32),
            jax.ShapeDtypeStruct((TABLE_ROWS, HALF), F32),
        ),
        in_specs=[smem, smem, vmem, vmem, vmem],
        out_specs=(vmem, vmem),
    )(routing, triple_modes, pes_grids, modals, energies)
    received = lax.all_to_all(pay, "exc", split_axis=0, concat_axis=0, tiled=True)
    for step in XOR_STEPS:
        other = lax.ppermute(table, "trip", [(n, n ^ step) for n in range(TRIPS)])
        table = jnp.concatenate([table, other], axis=0)

    return late_call(
        block_source, live_rows, received, table, spectator_energy, trial_vectors
    )


def solution(mesh):
    in_specs = (
        P(("trip", "exc"), None, None),
        P("trip", None),
        P("trip", None),
        P(("trip", "exc"), None),
        P("trip", None, "exc"),
        P(("trip", "exc")),
        P(("trip", "exc")),
        P(("trip", "exc"), None, None),
        P(("trip", "exc"), None),
    )
    out_specs = P(("trip", "exc"), None, None)
    return jax.shard_map(
        on_device, mesh=mesh, in_specs=in_specs, out_specs=out_specs, check_vma=False
    )
```

```python
import jax
import jax.numpy as jnp
from jax import lax
from jax.experimental import pallas as pl
from jax.experimental.pallas import tpu as pltpu
from jax.sharding import PartitionSpec as P

NMOD = 8
G = 16
NVEC = 64
S = 512
HALF = 256
COLS = 16
TRIPS = 8
TABLE_ROWS = 40
MODAL_ROWS = 32
PAY_ROWS = 32
XOR_STEPS = (1, 2, 6)
F32 = jnp.float32
BF16 = jnp.bfloat16


def iota(shape, axis):
    return lax.broadcasted_iota(jnp.int32, shape, axis)


def pack_kernel(routing, triple_modes, pes, modals, energies, pay, table):
    lane = iota((8, HALF), 1)
    per = modals.shape[0]
    for q in range(COLS):
        local = routing[q]
        pay[q, 0:G, :] = pes[local]
        names = jnp.zeros((8, HALF), F32)
        for n in range(3):
            mode = triple_modes[local, n]
            owner = lax.div(mode, per)
            names = jnp.where(lane == n, owner.astype(F32), names)
            names = jnp.where(lane == 3 + n, (mode - owner * per).astype(F32), names)
        pay[q, G : G + 8, :] = names
    table[...] = jnp.zeros_like(table)
    table[0:per, :] = modals[...]
    table[MODAL_ROWS:TABLE_ROWS, 0:per] = energies[...]


def split(x):
    high = x.astype(BF16)
    return high, (x - high.astype(F32)).astype(BF16)


def pick(values, chosen):
    high, low = split(values)
    return jnp.dot(high, chosen, preferred_element_type=F32) + jnp.dot(
        low, chosen, preferred_element_type=F32
    )


def ones_where(condition):
    return jnp.where(condition, 1.0, 0.0).astype(BF16)


def repeat_rows(x, count):
    rows, lanes = x.shape
    return jnp.broadcast_to(x[:, None, :], (rows, count, lanes)).reshape(rows * count, lanes)


def sigma_kernel(
    sources_live, pay, table, spectator, vectors, out,
    held, matrix, zeros, modal_i, modal_j, modal_k, modal_f, level, spread, used, in_sem, out_sem,
):
    blocks = held.shape[0]
    left, right = pl.ds(0, HALF), pl.ds(HALF, HALF)
    sources, live = sources_live.at[0], sources_live.at[1]

    def load(b, half, n):
        return pltpu.make_async_copy(vectors.at[b, :, half], held.at[b, :, half], in_sem.at[b, n])

    def store(b, half, n):
        return pltpu.make_async_copy(held.at[b, :, half], out.at[b, :, half], out_sem.at[b, n])

    def blank(b):
        return pltpu.make_async_copy(zeros, out.at[b, :, right], out_sem.at[b, 1])

    zeros[...] = jnp.zeros_like(zeros)
    for s in range(COLS):
        used[s] = 0

    @pl.loop(0, blocks)
    def _(b):
        used[sources[b]] = 1
        load(b, left, 0).start()

        @pl.when(live[b] > 4)
        def _():
            load(b, right, 1).start()

    @pl.loop(0, blocks)
    def _(b):
        @pl.when(live[b] <= 4)
        def _():
            blank(b).start()

    me = lax.axis_index("trip")


    def owner_of(slot):
        return (me ^ (slot & 3) ^ jnp.where((slot & 4) > 0, 6, 0)).astype(F32)

    owner = owner_of(iota((1, HALF), 1) // MODAL_ROWS)
    within = (iota((1, HALF), 1) % MODAL_ROWS).astype(F32)
    named = pay[:, G, :]
    owners = [named[:, n : n + 1] for n in range(3)]
    places = [named[:, n + 3 : n + 4] for n in range(3)]
    chosen = jnp.concatenate(
        [ones_where((owners[n] == owner) & (places[n] == within)) for n in range(3)], axis=0
    )
    starts = range(0, table.shape[0], TABLE_ROWS)
    modals = jnp.concatenate([table[n : n + MODAL_ROWS, :] for n in starts], axis=0)
    levels = jnp.concatenate([table[n + MODAL_ROWS : n + TABLE_ROWS, :] for n in starts], axis=0)
    levels = jnp.concatenate([levels, jnp.zeros_like(levels)], axis=0)
    high, low = split(modals)
    rows = jnp.dot(chosen, high, preferred_element_type=F32) + jnp.dot(
        chosen, low, preferred_element_type=F32
    )
    own_modal = iota((128, 128), 1) // G == iota((128, 128), 0) % NMOD
    first, second, third = (
        jnp.where(own_modal, repeat_rows(rows[16 * n : 16 * n + 16], NMOD), 0.0)
        for n in range(3)
    )
    by_major = ones_where(iota((128, HALF), 1) // G == iota((128, HALF), 0) % G)
    by_minor = ones_where(iota((128, HALF), 1) % G == iota((128, HALF), 0) % G)
    modal_i[...] = pick(first, by_major)
    modal_j[...] = pick(second, by_major)
    modal_k[...] = pick(third, by_minor)
    own_point = iota((HALF, 128), 1) % G == iota((HALF, 128), 0) % G
    points = jnp.where(own_point, repeat_rows(rows[0:16], G), 0.0)
    modal_f[...] = pick(points, ones_where(iota((128, S), 0) // G == iota((128, S), 1) // NVEC))
    row, col = iota((128, S), 0), iota((128, S), 1)
    level_high, level_low = split(levels)
    lane = iota((1, 128), 1)
    level_owner = jnp.where(lane < 64, owner_of(lane // NMOD), -1.0)
    total = jnp.zeros((COLS, S), F32)
    for n, digit in enumerate((col // 64, (col // 8) % 8, col % 8)):
        at = ones_where(places[n] == lane.astype(F32))
        found = lax.dot_general(
            at, level_high, (((1,), (1,)), ((), ())), preferred_element_type=F32
        ) + lax.dot_general(at, level_low, (((1,), (1,)), ((), ())), preferred_element_type=F32)
        own = jnp.where(owners[n] == level_owner, found, 0.0)
        total = total + pick(own, ones_where(row % NMOD == digit))
    level[...] = total
    padded = jnp.concatenate([spectator[...], jnp.zeros((blocks, 120), F32)], axis=1)
    spread[...] = pick(padded, ones_where(row == col // NVEC))

    same = iota((128, HALF), 0) % G == iota((128, HALF), 1) % G

    @pl.loop(0, COLS)
    def _(s):
        @pl.when(used[s] > 0)
        def _():
            eight = pl.ds(pl.multiple_of(s * 8, 8), 8)
            sixteen = pl.ds(pl.multiple_of(s * 16, 16), 16)
            grid = pay[s, 0:G, :]
            pairs = (modal_j[eight, :][:, None, :] * modal_k[eight, :][None, :, :]).reshape(64, HALF)
            high, low = split(pairs)
            weights = jnp.concatenate([high, high, low, low], axis=0)
            mix = jnp.where(same, repeat_rows(modal_i[eight, :], G), 0.0).astype(BF16)
            factor = modal_f[sixteen, :]
            levels = level[pl.ds(s, 1), :]
            for r in range(4):
                part = pairs[16 * r : 16 * r + 16]
                scaled = (grid[:, None, :] * part[None, :, :]).reshape(HALF, HALF).astype(BF16)
                both = lax.dot_general(
                    scaled, weights, (((1,), (1,)), ((), ())), preferred_element_type=F32
                )
                inner = (both[:, 0:128] + both[:, 128:256]).reshape(G, G, 128)
                wide = jnp.concatenate(
                    [
                        (inner * factor[:, None, 128 * j : 128 * j + 128])
                        .reshape(HALF, 128)
                        .astype(BF16)
                        for j in range(4)
                    ],
                    axis=1,
                )
                block = jnp.dot(mix, wide, preferred_element_type=F32)
                for a in range(NMOD):
                    tile = slice(128 * (a // 2), 128 * (a // 2) + 128)
                    at = iota((G, 128), 1) == iota((G, 128), 0) + (64 * (a % 2) + 16 * r)
                    mine = block[16 * a : 16 * a + 16, :]
                    target = slice(64 * a + 16 * r, 64 * a + 16 * r + 16)
                    matrix[s, target, :] = mine.astype(BF16)
                    matrix[s, target, tile] = (
                        mine[:, tile] + jnp.where(at, levels[:, tile], 0.0)
                    ).astype(BF16)

    def apply(b, lanes):
        coeff = held[b, :, 0:lanes]
        product = jnp.dot(matrix[sources[b]], coeff, preferred_element_type=F32)
        summed = product + spread[pl.ds(b, 1), 0:lanes] * coeff.astype(F32)
        kept = iota((1, lanes), 1) < live[b] * NVEC
        held[b, :, 0:lanes] = jnp.where(kept, summed, 0.0).astype(BF16)

    @pl.loop(0, blocks)
    def _(b):
        load(b, left, 0).wait()

        @pl.when(live[b] > 4)
        def _():
            load(b, right, 1).wait()
            apply(b, S)
            store(b, right, 1).start()

        @pl.when(live[b] <= 4)
        def _():
            apply(b, HALF)

        store(b, left, 0).start()

    @pl.loop(0, blocks)
    def _(b):
        store(b, left, 0).wait()
        store(b, right, 1).wait()


def late_call(sources, live, received, table, spectator, vectors):
    vmem, smem = pl.BlockSpec(memory_space=pltpu.VMEM), pl.BlockSpec(memory_space=pltpu.SMEM)
    anywhere = pl.BlockSpec(memory_space=pl.ANY)
    blocks = vectors.shape[0]
    return pl.pallas_call(
        sigma_kernel,
        out_shape=jax.ShapeDtypeStruct(vectors.shape, BF16),
        in_specs=[smem, vmem, vmem, vmem, anywhere],
        out_specs=anywhere,
        scratch_shapes=[
            pltpu.VMEM((blocks, S, S), BF16),
            pltpu.VMEM((COLS, S, S), BF16),
            pltpu.VMEM((S, HALF), BF16),
            pltpu.VMEM((128, HALF), F32),
            pltpu.VMEM((128, HALF), F32),
            pltpu.VMEM((128, HALF), F32),
            pltpu.VMEM((HALF, S), F32),
            pltpu.VMEM((COLS, S), F32),
            pltpu.VMEM((blocks, S), F32),
            pltpu.SMEM((COLS,), jnp.int32),
            pltpu.SemaphoreType.DMA((blocks, 2)),
            pltpu.SemaphoreType.DMA((blocks, 2)),
        ],
        compiler_params=pltpu.CompilerParams(vmem_limit_bytes=48 * 2**20),
        cost_estimate=pl.CostEstimate(
            flops=2 * (blocks + COLS) * S**3, bytes_accessed=4 * blocks * S * S, transcendentals=0
        ),
    )(jnp.stack([sources, live]), received, table, spectator, vectors)


def on_device(
    pes_grids,
    modals,
    energies,
    triple_modes,
    routing,
    block_source,
    live_rows,
    trial_vectors,
    spectator_energy,
):
    vmem, smem = pl.BlockSpec(memory_space=pltpu.VMEM), pl.BlockSpec(memory_space=pltpu.SMEM)
    pay, table = pl.pallas_call(
        pack_kernel,
        out_shape=(
            jax.ShapeDtypeStruct((COLS, PAY_ROWS, HALF), F32),
            jax.ShapeDtypeStruct((TABLE_ROWS, 128), F32),
        ),
        in_specs=[smem, smem, vmem, vmem, vmem],
        out_specs=(vmem, vmem),
    )(routing.reshape(COLS), triple_modes, pes_grids, modals, energies.T)
    received = lax.all_to_all(pay, "exc", split_axis=0, concat_axis=0, tiled=True)
    for step in XOR_STEPS:
        other = lax.ppermute(table, "trip", [(n, n ^ step) for n in range(TRIPS)])
        table = jnp.concatenate([table, other], axis=0)

    return late_call(
        block_source, live_rows, received, table, spectator_energy, trial_vectors
    )


def solution(mesh):
    in_specs = (
        P(("trip", "exc"), None, None),
        P("trip", None),
        P("trip", None),
        P(("trip", "exc"), None),
        P("trip", None, "exc"),
        P(("trip", "exc")),
        P(("trip", "exc")),
        P(("trip", "exc"), None, None),
        P(("trip", "exc"), None),
    )
    out_specs = P(("trip", "exc"), None, None)
    return jax.shard_map(
        on_device, mesh=mesh, in_specs=in_specs, out_specs=out_specs, check_vma=False
    )
```

```python
import jax
import jax.numpy as jnp
from jax import lax
from jax.experimental import pallas as pl
from jax.experimental.pallas import tpu as pltpu
from jax.sharding import PartitionSpec as P

NMOD = 8
G = 16
NVEC = 64
S = 512
HALF = 256
COLS = 16
TRIPS = 8
TABLE_ROWS = 40
MODAL_ROWS = 32
PAY_ROWS = 24
UNROLL = 8
F32 = jnp.float32
BF16 = jnp.bfloat16


def iota(shape, axis):
    return lax.broadcasted_iota(jnp.int32, shape, axis)


def pack_kernel(routing, triple_modes, pes, modals, energies, pay, table):
    lane = iota((8, HALF), 1)
    per = modals.shape[0]
    for q in range(COLS):
        local = routing[q]
        pay[q, 0:G, :] = pes[local]
        names = jnp.zeros((8, HALF), F32)
        for n in range(3):
            mode = triple_modes[local, n]
            owner = lax.div(mode, per)
            names = jnp.where(lane == n, owner.astype(F32), names)
            names = jnp.where(lane == 3 + n, (mode - owner * per).astype(F32), names)
        pay[q, G : G + 8, :] = names
    table[...] = jnp.zeros_like(table)
    table[0:per, :] = modals[...]
    table[MODAL_ROWS:TABLE_ROWS, 0:per] = energies[...]


def split(x):
    high = x.astype(BF16)
    return high, (x - high.astype(F32)).astype(BF16)


def pick(values, chosen):
    high, low = split(values)
    return jnp.dot(high, chosen, preferred_element_type=F32) + jnp.dot(
        low, chosen, preferred_element_type=F32
    )


def ones_where(condition):
    return jnp.where(condition, 1.0, 0.0).astype(BF16)


def repeat_rows(x, count):
    rows, lanes = x.shape
    return jnp.broadcast_to(x[:, None, :], (rows, count, lanes)).reshape(rows * count, lanes)


def sigma_kernel(
    sources_live, pay, table_0, table_1, table_2, table_3, spectator, vectors, out,
    held, matrix, folded, summed, modal_j, modal_k, level, spread, used, in_sem, out_sem,
):
    blocks = held.shape[0]
    sources, live = sources_live.at[0], sources_live.at[1]

    def load(b, n):
        at = pl.ds(n * HALF, HALF)
        return pltpu.make_async_copy(vectors.at[b, :, at], held.at[b, :, at], in_sem.at[b, n])

    def store(b):
        return pltpu.make_async_copy(held.at[b], out.at[b], out_sem)

    for s in range(COLS):
        used[s] = 0

    @pl.loop(0, blocks)
    def _(b):
        used[sources[b]] = 1
        load(b, 0).start()

        @pl.when(live[b] > 4)
        def _():
            load(b, 1).start()

    me = lax.axis_index("trip")


    def owner_of(slot):
        return (me ^ (slot & 3) ^ jnp.where((slot & 4) > 0, 6, 0)).astype(F32)

    owner = owner_of(iota((1, HALF), 1) // MODAL_ROWS)
    within = (iota((1, HALF), 1) % MODAL_ROWS).astype(F32)
    named = pay[:, G, :]
    owners = [named[:, n : n + 1] for n in range(3)]
    places = [named[:, n + 3 : n + 4] for n in range(3)]
    chosen = jnp.concatenate(
        [ones_where((owners[n] == owner) & (places[n] == within)) for n in range(3)], axis=0
    )
    tables = [
        table[n : n + TABLE_ROWS, :]
        for table in (table_0, table_1, table_2, table_3)
        for n in (0, TABLE_ROWS)
    ]
    modals = jnp.concatenate([table[0:MODAL_ROWS] for table in tables], axis=0)
    levels = jnp.concatenate([table[MODAL_ROWS:] for table in tables], axis=0)
    levels = jnp.concatenate([levels, jnp.zeros_like(levels)], axis=0)
    high, low = split(modals)
    rows = jnp.dot(chosen, high, preferred_element_type=F32) + jnp.dot(
        chosen, low, preferred_element_type=F32
    )
    own_modal = iota((128, 128), 1) // G == iota((128, 128), 0) % NMOD
    first, second, third = (
        jnp.where(own_modal, repeat_rows(rows[16 * n : 16 * n + 16], NMOD), 0.0)
        for n in range(3)
    )
    by_major = ones_where(iota((128, HALF), 1) // G == iota((128, HALF), 0) % G)
    by_minor = ones_where(iota((128, HALF), 1) % G == iota((128, HALF), 0) % G)
    points = jnp.where(
        iota((128, HALF), 1) // G == iota((128, HALF), 0) // NMOD, pick(first, by_minor), 0.0
    ).reshape(COLS, NMOD, 1, HALF)
    squares = (points * points.reshape(COLS, 1, NMOD, HALF)).reshape(COLS * 64, HALF)
    high, low = split(squares)
    grid_high, grid_low = split(pay[:, 0:G, :].reshape(HALF, HALF))
    summed[...] = (
        jnp.dot(high, grid_high, preferred_element_type=F32)
        + jnp.dot(low, grid_high, preferred_element_type=F32)
        + jnp.dot(high, grid_low, preferred_element_type=F32)
    )
    modal_j[...] = pick(second, by_major)
    modal_k[...] = pick(third, by_minor)
    row, col = iota((128, 2 * S), 0), iota((128, 2 * S), 1)
    level_high, level_low = split(levels)
    lane = iota((1, 128), 1)
    level_owner = jnp.where(lane < 64, owner_of(lane // NMOD), -1.0)
    total = jnp.zeros((COLS, 2 * S), F32)
    for n, digit in enumerate((col // 128, (col // 8) % 8, col % 8)):
        at = ones_where(places[n] == lane.astype(F32))
        found = lax.dot_general(
            at, level_high, (((1,), (1,)), ((), ())), preferred_element_type=F32
        ) + lax.dot_general(at, level_low, (((1,), (1,)), ((), ())), preferred_element_type=F32)
        own = jnp.where(owners[n] == level_owner, found, 0.0)
        total = total + pick(own, ones_where(row % NMOD == digit))
    level[...] = total
    padded = jnp.concatenate([spectator[...], jnp.zeros((blocks, 120), F32)], axis=1)
    spread[...] = pick(padded, ones_where(iota((128, S), 0) == iota((128, S), 1) // NVEC))

    on_left = iota((64, 128), 1) < 64
    on_diagonal = iota((64, 128), 1) % 64 == iota((64, 128), 0)

    @pl.loop(0, COLS)
    def _(s):
        @pl.when(used[s] > 0)
        def _():
            eight = pl.ds(pl.multiple_of(s * 8, 8), 8)
            pairs = (modal_j[eight, :][:, None, :] * modal_k[eight, :][None, :, :]).reshape(64, HALF)
            half = pairs.astype(BF16)
            weights = jnp.concatenate([half, half], axis=0)
            levels = level[pl.ds(s, 1), :]
            place = {}
            for a in range(NMOD):
                others = NMOD - a
                grid = summed[pl.ds(pl.multiple_of(s * 64, 64) + a * NMOD, NMOD), :]
                scaled = (grid[a:, None, :] * pairs[None, :, :]).reshape(64 * others, HALF)
                blocks_of = lax.dot_general(
                    scaled.astype(BF16), weights, (((1,), (1,)), ((), ())), preferred_element_type=F32
                )
                for n in range(others):
                    place[a, a + n] = place[a + n, a] = 64 * (len(set(place.values())))
                    one = blocks_of[64 * n : 64 * n + 64, :]
                    if n == 0:
                        one = one + jnp.where(
                            on_diagonal, levels[:, 128 * a : 128 * a + 128], 0.0
                        )
                    at = place[a, a + n]
                    folded[at : at + 64, :] = one.astype(BF16)
            for a in range(NMOD):
                for j in range(NMOD // 2):
                    even, odd = place[a, 2 * j], place[a, 2 * j + 1]
                    matrix[s, j, 64 * a : 64 * a + 64, :] = jnp.where(
                        on_left, folded[even : even + 64, :], folded[odd : odd + 64, :]
                    )

    def product(b):
        whole = jnp.concatenate([matrix[sources[b], n] for n in range(4)], axis=1)
        return jnp.dot(whole, held[b], preferred_element_type=F32)

    def finish(b, block):
        scale = spread[pl.ds(b, 1), :]
        kept = iota((1, S), 1) < live[b] * NVEC
        summed_up = block + scale * held[b].astype(F32)
        held[b] = jnp.where(kept, summed_up, 0.0).astype(BF16)
        store(b).start()

    @pl.loop(0, blocks // UNROLL)
    def _(step):
        first = step * UNROLL
        for n in range(UNROLL):
            load(first + n, 0).wait()

            @pl.when(live[first + n] > 4)
            def _(n=n):
                load(first + n, 1).wait()

        block = product(first)
        for n in range(UNROLL):
            later = product(first + n + 1) if n + 1 < UNROLL else None
            finish(first + n, block)
            block = later

    pltpu.make_async_copy(held, out, out_sem).wait()


def late_call(sources, live, received, tables, spectator, vectors):
    vmem, smem = pl.BlockSpec(memory_space=pltpu.VMEM), pl.BlockSpec(memory_space=pltpu.SMEM)
    anywhere = pl.BlockSpec(memory_space=pl.ANY)
    blocks = vectors.shape[0]
    return pl.pallas_call(
        sigma_kernel,
        out_shape=jax.ShapeDtypeStruct(vectors.shape, BF16),
        in_specs=[smem, vmem, vmem, vmem, vmem, vmem, vmem, anywhere],
        out_specs=anywhere,
        scratch_shapes=[
            pltpu.VMEM((blocks, S, S), BF16),
            pltpu.VMEM((COLS, 4, S, 128), BF16),
            pltpu.VMEM((36 * 64, 128), BF16),
            pltpu.VMEM((COLS * 64, HALF), F32),
            pltpu.VMEM((128, HALF), F32),
            pltpu.VMEM((128, HALF), F32),
            pltpu.VMEM((COLS, 2 * S), F32),
            pltpu.VMEM((blocks, S), F32),
            pltpu.SMEM((COLS,), jnp.int32),
            pltpu.SemaphoreType.DMA((blocks, 2)),
            pltpu.SemaphoreType.DMA,
        ],
        compiler_params=pltpu.CompilerParams(vmem_limit_bytes=48 * 2**20),
        cost_estimate=pl.CostEstimate(
            flops=2 * (blocks + COLS) * S**3, bytes_accessed=4 * blocks * S * S, transcendentals=0
        ),
    )(jnp.stack([sources, live]), received, *tables, spectator, vectors)


def on_device(
    pes_grids,
    modals,
    energies,
    triple_modes,
    routing,
    block_source,
    live_rows,
    trial_vectors,
    spectator_energy,
):
    vmem, smem = pl.BlockSpec(memory_space=pltpu.VMEM), pl.BlockSpec(memory_space=pltpu.SMEM)
    pay, table = pl.pallas_call(
        pack_kernel,
        out_shape=(
            jax.ShapeDtypeStruct((COLS, PAY_ROWS, HALF), F32),
            jax.ShapeDtypeStruct((TABLE_ROWS, 128), F32),
        ),
        in_specs=[smem, smem, vmem, vmem, vmem],
        out_specs=(vmem, vmem),
    )(routing.reshape(COLS), triple_modes, pes_grids, modals, energies.T)
    received = lax.all_to_all(pay, "exc", split_axis=0, concat_axis=0, tiled=True)

    def swap(x, step):
        return lax.ppermute(x, "trip", [(n, n ^ step) for n in range(TRIPS)])

    both = jnp.concatenate([table, swap(table, 1)], axis=0)
    near, far = swap(both, 2), swap(both, 6)
    tables = (both, near, far, swap(near, 6))
    return late_call(
        block_source, live_rows, received, tables, spectator_energy, trial_vectors
    )


def solution(mesh):
    in_specs = (
        P(("trip", "exc"), None, None),
        P("trip", None),
        P("trip", None),
        P(("trip", "exc"), None),
        P("trip", None, "exc"),
        P(("trip", "exc")),
        P(("trip", "exc")),
        P(("trip", "exc"), None, None),
        P(("trip", "exc"), None),
    )
    out_specs = P(("trip", "exc"), None, None)
    return jax.shard_map(
        on_device, mesh=mesh, in_specs=in_specs, out_specs=out_specs, check_vma=False
    )
```

```python
import jax
import jax.numpy as jnp
from jax import lax
from jax.experimental import pallas as pl
from jax.experimental.pallas import tpu as pltpu
from jax.sharding import PartitionSpec as P

NMOD = 8
G = 16
NVEC = 64
S = 512
HALF = 256
COLS = 16
TRIPS = 8
TABLE_ROWS = 40
MODAL_ROWS = 32
PAY_ROWS = 24
UNROLL = 8
F32 = jnp.float32
BF16 = jnp.bfloat16


def iota(shape, axis):
    return lax.broadcasted_iota(jnp.int32, shape, axis)


def pack_kernel(routing, triple_modes, pes, modals, energies, pay, table):
    lane = iota((8, HALF), 1)
    per = modals.shape[0]
    for q in range(COLS):
        local = routing[q]
        pay[q, 0:G, :] = pes[local]
        names = jnp.zeros((8, HALF), F32)
        for n in range(3):
            mode = triple_modes[local, n]
            owner = lax.div(mode, per)
            names = jnp.where(lane == n, owner.astype(F32), names)
            names = jnp.where(lane == 3 + n, (mode - owner * per).astype(F32), names)
        pay[q, G : G + 8, :] = names
    table[...] = jnp.zeros_like(table)
    table[0:per, :] = modals[...]
    table[MODAL_ROWS:TABLE_ROWS, 0:per] = energies[...]


def split(x):
    high = x.astype(BF16)
    return high, (x - high.astype(F32)).astype(BF16)


def pick(values, chosen):
    both = jnp.concatenate(split(values), axis=1)
    return jnp.dot(both, jnp.concatenate([chosen, chosen], axis=0), preferred_element_type=F32)


def ones_where(condition):
    return jnp.where(condition, 1.0, 0.0).astype(BF16)


def repeat_rows(x, count):
    rows, lanes = x.shape
    return jnp.broadcast_to(x[:, None, :], (rows, count, lanes)).reshape(rows * count, lanes)


def sigma_kernel(
    sources_live, pay, table_0, table_1, table_2, table_3, spectator, vectors, out,
    held, matrix, folded, summed, modal_j, modal_k, level, spread, used, order, in_sem, out_sem,
):
    blocks = held.shape[0]
    sources, live = sources_live.at[0], sources_live.at[1]

    def load(b):
        return pltpu.make_async_copy(vectors.at[b], held.at[b], in_sem.at[b])

    def store(b):
        return pltpu.make_async_copy(held.at[b], out.at[b], out_sem)

    for s in range(COLS):
        used[s] = 0

    @pl.loop(0, blocks)
    def _(b):
        used[sources[b]] = 1
        load(b).start()

    me = lax.axis_index("trip")


    def owner_of(slot):
        return (me ^ (slot & 3) ^ jnp.where((slot & 4) > 0, 6, 0)).astype(F32)

    owner = owner_of(iota((1, HALF), 1) // MODAL_ROWS)
    within = (iota((1, HALF), 1) % MODAL_ROWS).astype(F32)
    named = pay[:, G, :]
    owners = [named[:, n : n + 1] for n in range(3)]
    places = [named[:, n + 3 : n + 4] for n in range(3)]
    chosen = jnp.concatenate(
        [ones_where((owners[n] == owner) & (places[n] == within)) for n in range(3)], axis=0
    )
    tables = [
        table[n : n + TABLE_ROWS, :]
        for table in (table_0, table_1, table_2, table_3)
        for n in (0, TABLE_ROWS)
    ]
    modals = jnp.concatenate([table[0:MODAL_ROWS] for table in tables], axis=0)
    levels = jnp.concatenate([table[MODAL_ROWS:] for table in tables], axis=0)
    levels = jnp.concatenate([levels, jnp.zeros_like(levels)], axis=0)
    high, low = split(modals)
    rows = jnp.dot(chosen, high, preferred_element_type=F32) + jnp.dot(
        chosen, low, preferred_element_type=F32
    )
    own_modal = iota((128, 128), 1) // G == iota((128, 128), 0) % NMOD
    first, second, third = (
        jnp.where(own_modal, repeat_rows(rows[16 * n : 16 * n + 16], NMOD), 0.0)
        for n in range(3)
    )
    by_major = ones_where(iota((128, HALF), 1) // G == iota((128, HALF), 0) % G)
    by_minor = ones_where(iota((128, HALF), 1) % G == iota((128, HALF), 0) % G)
    modal_i = pick(first, by_minor[:, 0:128])
    part = iota((64, 128), 1) // G
    empty = jnp.zeros((128 - 3 * G, HALF), BF16)
    for n in range(COLS):
        mine = modal_i[8 * n : 8 * n + 8]
        high, low = split((mine[:, None, :] * mine[None, :, :]).reshape(64, 128))
        squares = jnp.where(part == 1, low.astype(F32), jnp.where(part < 3, high.astype(F32), 0.0))
        grid_high, grid_low = split(pay[n, 0:G, :])
        grids = jnp.concatenate([grid_high, grid_high, grid_low, empty], axis=0)
        summed[64 * n : 64 * n + 64, :] = jnp.dot(
            squares.astype(BF16), grids, preferred_element_type=F32
        )
    modal_j[...] = pick(second, by_major)
    modal_k[...] = pick(third, by_minor)
    level_high, level_low = split(levels)
    table_levels = jnp.concatenate([level_high, level_low], axis=0)
    lane = iota((1, 128), 1)
    level_owner = jnp.where(lane < 64, owner_of(lane // NMOD), -1.0)
    row, col = iota((128, 128), 0), iota((128, 128), 1)
    parts = []
    for n, digit in enumerate((col % 8, (col // 8) % 8, col % 8)):
        at = ones_where(places[n] == lane.astype(F32))
        found = lax.dot_general(
            at, table_levels, (((1,), (1,)), ((), ())), preferred_element_type=F32
        )
        own = jnp.where(owners[n] == level_owner, found[:, 0:128] + found[:, 128:256], 0.0)
        parts.append(pick(own, ones_where(row % NMOD == digit)))
    rest = parts[1] + parts[2]
    for a in range(NMOD):
        level[:, 128 * a : 128 * a + 128] = rest + parts[0][:, a : a + 1]
    padded = jnp.concatenate([spectator[...], jnp.zeros((blocks, 120), F32)], axis=1)
    spread[...] = pick(padded, ones_where(iota((128, S), 0) == iota((128, S), 1) // NVEC))

    on_left = iota((64, 128), 1) < 64
    on_diagonal = iota((64, 128), 1) % 64 == iota((64, 128), 0)
    combos = [(a, n) for a in range(NMOD) for n in range(a, NMOD)]
    place = {c: 64 * i for i, c in enumerate(combos)}
    place |= {(n, a): at for (a, n), at in place.items()}

    def build(s, spot):
        eight = pl.ds(pl.multiple_of(s * 8, 8), 8)
        pairs = (modal_j[eight, :][:, None, :] * modal_k[eight, :][None, :, :]).reshape(64, HALF)
        half = pairs.astype(BF16)
        weights = jnp.concatenate([half, half], axis=0)
        levels = level[pl.ds(s, 1), :]
        grids = [
            summed[pl.ds(pl.multiple_of(s * 64, 64) + a * NMOD, NMOD), :] for a in range(NMOD)
        ]
        scaled = [(grids[a][n : n + 1] * pairs).astype(BF16) for a, n in combos]
        whole = lax.dot_general(
            jnp.concatenate(scaled, axis=0),
            weights,
            (((1,), (1,)), ((), ())),
            preferred_element_type=F32,
        )
        for i, (a, n) in enumerate(combos):
            one = whole[64 * i : 64 * i + 64, :]
            if a == n:
                one = one + jnp.where(on_diagonal, levels[:, 128 * a : 128 * a + 128], 0.0)
            folded[spot, 64 * i : 64 * i + 64, :] = one.astype(BF16)

    def spread_out(s, spot):
        for a in range(NMOD):
            for j in range(NMOD // 2):
                even, odd = place[a, 2 * j], place[a, 2 * j + 1]
                matrix[s, j, 64 * a : 64 * a + 64, :] = jnp.where(
                    on_left, folded[spot, even : even + 64, :], folded[spot, odd : odd + 64, :]
                )

    count = jnp.int32(0)
    for s in range(COLS):
        order[count] = s
        count = count + used[s]
    order[count] = order[jnp.maximum(count - 1, 0)]

    @pl.loop(0, (count + 1) // 2)
    def _(step):
        here, there = order[2 * step], order[2 * step + 1]
        build(here, 0)
        build(there, 1)
        spread_out(here, 0)
        spread_out(there, 1)

    def product(b):
        whole = jnp.concatenate([matrix[sources[b], n] for n in range(4)], axis=1)
        return jnp.dot(whole, held[b], preferred_element_type=F32)

    def finish(b, block):
        scale = spread[pl.ds(b, 1), :]
        kept = ones_where(iota((1, S), 1) < live[b] * NVEC)
        held[b] = (block + scale * held[b].astype(F32)).astype(BF16) * kept
        store(b).start()

    @pl.loop(0, blocks // UNROLL)
    def _(step):
        first = step * UNROLL
        for n in range(UNROLL):
            load(first + n).wait()

        block = product(first)
        for n in range(UNROLL):
            later = product(first + n + 1) if n + 1 < UNROLL else None
            finish(first + n, block)
            block = later

    pltpu.make_async_copy(held, out, out_sem).wait()


def late_call(sources, live, received, tables, spectator, vectors):
    vmem, smem = pl.BlockSpec(memory_space=pltpu.VMEM), pl.BlockSpec(memory_space=pltpu.SMEM)
    anywhere = pl.BlockSpec(memory_space=pl.ANY)
    blocks = vectors.shape[0]
    return pl.pallas_call(
        sigma_kernel,
        out_shape=jax.ShapeDtypeStruct(vectors.shape, BF16),
        in_specs=[smem, vmem, vmem, vmem, vmem, vmem, vmem, anywhere],
        out_specs=anywhere,
        scratch_shapes=[
            pltpu.VMEM((blocks, S, S), BF16),
            pltpu.VMEM((COLS, 4, S, 128), BF16),
            pltpu.VMEM((2, 36 * 64, 128), BF16),
            pltpu.VMEM((COLS * 64, HALF), F32),
            pltpu.VMEM((128, HALF), F32),
            pltpu.VMEM((128, HALF), F32),
            pltpu.VMEM((COLS, 2 * S), F32),
            pltpu.VMEM((blocks, S), F32),
            pltpu.SMEM((COLS,), jnp.int32),
            pltpu.SMEM((COLS + 1,), jnp.int32),
            pltpu.SemaphoreType.DMA((blocks,)),
            pltpu.SemaphoreType.DMA,
        ],
        compiler_params=pltpu.CompilerParams(vmem_limit_bytes=48 * 2**20),
        cost_estimate=pl.CostEstimate(
            flops=2 * (blocks + COLS) * S**3, bytes_accessed=4 * blocks * S * S, transcendentals=0
        ),
    )(jnp.stack([sources, live]), received, *tables, spectator, vectors)


def on_device(
    pes_grids,
    modals,
    energies,
    triple_modes,
    routing,
    block_source,
    live_rows,
    trial_vectors,
    spectator_energy,
):
    vmem, smem = pl.BlockSpec(memory_space=pltpu.VMEM), pl.BlockSpec(memory_space=pltpu.SMEM)
    pay, table = pl.pallas_call(
        pack_kernel,
        out_shape=(
            jax.ShapeDtypeStruct((COLS, PAY_ROWS, HALF), F32),
            jax.ShapeDtypeStruct((TABLE_ROWS, 128), F32),
        ),
        in_specs=[smem, smem, vmem, vmem, vmem],
        out_specs=(vmem, vmem),
    )(routing.reshape(COLS), triple_modes, pes_grids, modals, energies.T)
    received = lax.all_to_all(pay, "exc", split_axis=0, concat_axis=0, tiled=True)

    def swap(x, step):
        return lax.ppermute(x, "trip", [(n, n ^ step) for n in range(TRIPS)])

    both = jnp.concatenate([table, swap(table, 1)], axis=0)
    near, far = swap(both, 2), swap(both, 6)
    tables = (both, near, far, swap(near, 6))
    return late_call(
        block_source, live_rows, received, tables, spectator_energy, trial_vectors
    )


def solution(mesh):
    in_specs = (
        P(("trip", "exc"), None, None),
        P("trip", None),
        P("trip", None),
        P(("trip", "exc"), None),
        P("trip", None, "exc"),
        P(("trip", "exc")),
        P(("trip", "exc")),
        P(("trip", "exc"), None, None),
        P(("trip", "exc"), None),
    )
    out_specs = P(("trip", "exc"), None, None)
    return jax.shard_map(
        on_device, mesh=mesh, in_specs=in_specs, out_specs=out_specs, check_vma=False
    )
```

```python
import jax
import jax.numpy as jnp
from jax import lax
from jax.experimental import pallas as pl
from jax.experimental.pallas import tpu as pltpu
from jax.sharding import PartitionSpec as P

NMOD = 8
G = 16
NVEC = 64
S = 512
HALF = 256
COLS = 16
TRIPS = 8
TABLE_ROWS = 40
MODAL_ROWS = 32
PAY_ROWS = 24
UNROLL = 12
F32 = jnp.float32
BF16 = jnp.bfloat16


def iota(shape, axis):
    return lax.broadcasted_iota(jnp.int32, shape, axis)


def pack_kernel(routing, triple_modes, pes, modals, energies, pay, table):
    lane = iota((8, HALF), 1)
    per = modals.shape[0]
    for q in range(COLS):
        local = routing[q]
        pay[q, 0:G, :] = pes[local]
        names = jnp.zeros((8, HALF), F32)
        for n in range(3):
            mode = triple_modes[local, n]
            owner = lax.div(mode, per)
            names = jnp.where(lane == n, owner.astype(F32), names)
            names = jnp.where(lane == 3 + n, (mode - owner * per).astype(F32), names)
        pay[q, G : G + 8, :] = names
    table[...] = jnp.zeros_like(table)
    table[0:per, :] = modals[...]
    table[MODAL_ROWS:TABLE_ROWS, 0:per] = energies[...]


def split(x):
    high = x.astype(BF16)
    return high, (x - high.astype(F32)).astype(BF16)


def pick(values, chosen):
    both = jnp.concatenate(split(values), axis=1)
    return jnp.dot(both, jnp.concatenate([chosen, chosen], axis=0), preferred_element_type=F32)


def ones_where(condition):
    return jnp.where(condition, 1.0, 0.0).astype(BF16)


def repeat_rows(x, count):
    rows, lanes = x.shape
    return jnp.broadcast_to(x[:, None, :], (rows, count, lanes)).reshape(rows * count, lanes)


def sigma_kernel(
    sources_live, pay, table_0, table_1, table_2, table_3, spectator, vectors, out,
    held, matrix, folded, summed, modal_j, modal_k, level, spread, used, order, in_sem, out_sem,
):
    blocks = held.shape[0]
    sources, live = sources_live.at[0], sources_live.at[1]

    def load(b):
        return pltpu.make_async_copy(vectors.at[b], held.at[b], in_sem.at[b])

    def store(b):
        return pltpu.make_async_copy(held.at[b], out.at[b], out_sem)

    for s in range(COLS):
        used[s] = 0

    @pl.loop(0, blocks)
    def _(b):
        used[sources[b]] = 1
        load(b).start()

    me = lax.axis_index("trip")


    def owner_of(slot):
        return (me ^ (slot & 3) ^ jnp.where((slot & 4) > 0, 6, 0)).astype(F32)

    owner = owner_of(iota((1, HALF), 1) // MODAL_ROWS)
    within = (iota((1, HALF), 1) % MODAL_ROWS).astype(F32)
    named = pay[:, G, :]
    owners = [named[:, n : n + 1] for n in range(3)]
    places = [named[:, n + 3 : n + 4] for n in range(3)]
    chosen = jnp.concatenate(
        [ones_where((owners[n] == owner) & (places[n] == within)) for n in range(3)], axis=0
    )
    tables = [
        table[n : n + TABLE_ROWS, :]
        for table in (table_0, table_1, table_2, table_3)
        for n in (0, TABLE_ROWS)
    ]
    modals = jnp.concatenate([table[0:MODAL_ROWS] for table in tables], axis=0)
    levels = jnp.concatenate([table[MODAL_ROWS:] for table in tables], axis=0)
    levels = jnp.concatenate([levels, jnp.zeros_like(levels)], axis=0)
    high, low = split(modals)
    rows = jnp.dot(chosen, high, preferred_element_type=F32) + jnp.dot(
        chosen, low, preferred_element_type=F32
    )
    own_modal = iota((128, 128), 1) // G == iota((128, 128), 0) % NMOD
    first, second, third = (
        jnp.where(own_modal, repeat_rows(rows[16 * n : 16 * n + 16], NMOD), 0.0)
        for n in range(3)
    )
    by_major = ones_where(iota((128, HALF), 1) // G == iota((128, HALF), 0) % G)
    by_minor = ones_where(iota((128, HALF), 1) % G == iota((128, HALF), 0) % G)
    modal_i = pick(first, by_minor[:, 0:128])
    part = iota((64, 128), 1) // G
    empty = jnp.zeros((128 - 3 * G, HALF), BF16)
    for n in range(COLS):
        mine = modal_i[8 * n : 8 * n + 8]
        high, low = split((mine[:, None, :] * mine[None, :, :]).reshape(64, 128))
        squares = jnp.where(part == 1, low.astype(F32), jnp.where(part < 3, high.astype(F32), 0.0))
        grid_high, grid_low = split(pay[n, 0:G, :])
        grids = jnp.concatenate([grid_high, grid_high, grid_low, empty], axis=0)
        summed[64 * n : 64 * n + 64, :] = jnp.dot(
            squares.astype(BF16), grids, preferred_element_type=F32
        )
    modal_j[...] = pick(second, by_major)
    modal_k[...] = pick(third, by_minor)
    level_high, level_low = split(levels)
    table_levels = jnp.concatenate([level_high, level_low], axis=0)
    lane = iota((1, 128), 1)
    level_owner = jnp.where(lane < 64, owner_of(lane // NMOD), -1.0)
    row, col = iota((128, 128), 0), iota((128, 128), 1)
    parts = []
    for n, digit in enumerate((col % 8, (col // 8) % 8, col % 8)):
        at = ones_where(places[n] == lane.astype(F32))
        found = lax.dot_general(
            at, table_levels, (((1,), (1,)), ((), ())), preferred_element_type=F32
        )
        own = jnp.where(owners[n] == level_owner, found[:, 0:128] + found[:, 128:256], 0.0)
        parts.append(pick(own, ones_where(row % NMOD == digit)))
    rest = parts[1] + parts[2]
    for a in range(NMOD):
        level[:, 128 * a : 128 * a + 128] = rest + parts[0][:, a : a + 1]
    padded = jnp.concatenate([spectator[...], jnp.zeros((blocks, 120), F32)], axis=1)
    spread[...] = pick(padded, ones_where(iota((128, S), 0) == iota((128, S), 1) // NVEC))

    on_left = iota((64, 128), 1) < 64
    on_diagonal = iota((64, 128), 1) % 64 == iota((64, 128), 0)
    combos = [(a, n) for a in range(NMOD) for n in range(a, NMOD)]
    place = {c: 64 * i for i, c in enumerate(combos)}
    place |= {(n, a): at for (a, n), at in place.items()}

    def build(s, spot):
        eight = pl.ds(pl.multiple_of(s * 8, 8), 8)
        pairs = (modal_j[eight, :][:, None, :] * modal_k[eight, :][None, :, :]).reshape(64, HALF)
        half = pairs.astype(BF16)
        weights = jnp.concatenate([half, half], axis=0)
        levels = level[pl.ds(s, 1), :]
        grids = [
            summed[pl.ds(pl.multiple_of(s * 64, 64) + a * NMOD, NMOD), :] for a in range(NMOD)
        ]
        scaled = [(grids[a][n : n + 1] * pairs).astype(BF16) for a, n in combos]
        whole = lax.dot_general(
            jnp.concatenate(scaled, axis=0),
            weights,
            (((1,), (1,)), ((), ())),
            preferred_element_type=F32,
        )
        for i, (a, n) in enumerate(combos):
            one = whole[64 * i : 64 * i + 64, :]
            if a == n:
                one = one + jnp.where(on_diagonal, levels[:, 128 * a : 128 * a + 128], 0.0)
            folded[spot, 64 * i : 64 * i + 64, :] = one.astype(BF16)

    def spread_out(s, spot):
        for a in range(NMOD):
            for j in range(NMOD // 2):
                even, odd = place[a, 2 * j], place[a, 2 * j + 1]
                matrix[s, j, 64 * a : 64 * a + 64, :] = jnp.where(
                    on_left, folded[spot, even : even + 64, :], folded[spot, odd : odd + 64, :]
                )

    count = jnp.int32(0)
    for s in range(COLS):
        order[count] = s
        count = count + used[s]
    order[count] = order[jnp.maximum(count - 1, 0)]

    @pl.loop(0, (count + 1) // 2)
    def _(step):
        here, there = order[2 * step], order[2 * step + 1]
        build(here, 0)
        build(there, 1)
        spread_out(here, 0)
        spread_out(there, 1)

    def product(b):
        whole = jnp.concatenate([matrix[sources[b], n] for n in range(4)], axis=1)
        return jnp.dot(whole, held[b], preferred_element_type=F32)

    def finish(b, block):
        scale = spread[pl.ds(b, 1), :]
        kept = ones_where(iota((1, S), 1) < live[b] * NVEC)
        held[b] = (block + scale * held[b].astype(F32)).astype(BF16) * kept
        store(b).start()

    @pl.loop(0, blocks // UNROLL)
    def _(step):
        first = step * UNROLL
        for n in range(UNROLL):
            load(first + n).wait()

        block = product(first)
        for n in range(UNROLL):
            later = product(first + n + 1) if n + 1 < UNROLL else None
            finish(first + n, block)
            block = later

    pltpu.make_async_copy(held, out, out_sem).wait()


def late_call(sources, live, received, tables, spectator, vectors):
    vmem, smem = pl.BlockSpec(memory_space=pltpu.VMEM), pl.BlockSpec(memory_space=pltpu.SMEM)
    anywhere = pl.BlockSpec(memory_space=pl.ANY)
    blocks = vectors.shape[0]
    return pl.pallas_call(
        sigma_kernel,
        out_shape=jax.ShapeDtypeStruct(vectors.shape, BF16),
        in_specs=[smem, vmem, vmem, vmem, vmem, vmem, vmem, anywhere],
        out_specs=anywhere,
        scratch_shapes=[
            pltpu.VMEM((blocks, S, S), BF16),
            pltpu.VMEM((COLS, 4, S, 128), BF16),
            pltpu.VMEM((2, 36 * 64, 128), BF16),
            pltpu.VMEM((COLS * 64, HALF), F32),
            pltpu.VMEM((128, HALF), F32),
            pltpu.VMEM((128, HALF), F32),
            pltpu.VMEM((COLS, 2 * S), F32),
            pltpu.VMEM((blocks, S), F32),
            pltpu.SMEM((COLS,), jnp.int32),
            pltpu.SMEM((COLS + 1,), jnp.int32),
            pltpu.SemaphoreType.DMA((blocks,)),
            pltpu.SemaphoreType.DMA,
        ],
        compiler_params=pltpu.CompilerParams(vmem_limit_bytes=48 * 2**20),
        cost_estimate=pl.CostEstimate(
            flops=2 * (blocks + COLS) * S**3, bytes_accessed=4 * blocks * S * S, transcendentals=0
        ),
    )(jnp.stack([sources, live]), received, *tables, spectator, vectors)


def on_device(
    pes_grids,
    modals,
    energies,
    triple_modes,
    routing,
    block_source,
    live_rows,
    trial_vectors,
    spectator_energy,
):
    vmem, smem = pl.BlockSpec(memory_space=pltpu.VMEM), pl.BlockSpec(memory_space=pltpu.SMEM)
    pay, table = pl.pallas_call(
        pack_kernel,
        out_shape=(
            jax.ShapeDtypeStruct((COLS, PAY_ROWS, HALF), F32),
            jax.ShapeDtypeStruct((TABLE_ROWS, 128), F32),
        ),
        in_specs=[smem, smem, vmem, vmem, vmem],
        out_specs=(vmem, vmem),
    )(routing.reshape(COLS), triple_modes, pes_grids, modals, energies.T)
    received = lax.all_to_all(pay, "exc", split_axis=0, concat_axis=0, tiled=True)

    def swap(x, step):
        return lax.ppermute(x, "trip", [(n, n ^ step) for n in range(TRIPS)])

    both = jnp.concatenate([table, swap(table, 1)], axis=0)
    near, far = swap(both, 2), swap(both, 6)
    tables = (both, near, far, swap(both, 4))
    return late_call(
        block_source, live_rows, received, tables, spectator_energy, trial_vectors
    )


def solution(mesh):
    in_specs = (
        P(("trip", "exc"), None, None),
        P("trip", None),
        P("trip", None),
        P(("trip", "exc"), None),
        P("trip", None, "exc"),
        P(("trip", "exc")),
        P(("trip", "exc")),
        P(("trip", "exc"), None, None),
        P(("trip", "exc"), None),
    )
    out_specs = P(("trip", "exc"), None, None)
    return jax.shard_map(
        on_device, mesh=mesh, in_specs=in_specs, out_specs=out_specs, check_vma=False
    )
```

```python
import jax
import jax.numpy as jnp
from jax import lax
from jax.experimental import pallas as pl
from jax.experimental.pallas import tpu as pltpu
from jax.sharding import PartitionSpec as P

NMOD = 8
G = 16
NVEC = 64
S = 512
HALF = 256
COLS = 16
TRIPS = 8
TABLE_ROWS = 40
MODAL_ROWS = 32
PAY_ROWS = 24
UNROLL = 12
F32 = jnp.float32
BF16 = jnp.bfloat16


def iota(shape, axis):
    return lax.broadcasted_iota(jnp.int32, shape, axis)


def pack_kernel(routing, triple_modes, pes, modals, energies, pay, table, names_of, sems):
    lane = iota((8, HALF), 1)
    per = modals.shape[0]

    def grids(q, local):
        return pltpu.make_async_copy(pes.at[local], pay.at[q, pl.ds(0, G), :], sems.at[q])

    naming = pltpu.make_async_copy(names_of, pay.at[:, pl.ds(G, 8), :], sems.at[COLS])
    for q in range(COLS):
        local = routing[q]
        grids(q, local).start()
        names = jnp.zeros((8, HALF), F32)
        for n in range(3):
            mode = triple_modes[local, n]
            owner = lax.div(mode, per)
            names = jnp.where(lane == n, owner.astype(F32), names)
            names = jnp.where(lane == 3 + n, (mode - owner * per).astype(F32), names)
        names_of[q] = names
    naming.start()
    table[...] = jnp.zeros_like(table)
    table[0:per, :] = modals[...]
    table[MODAL_ROWS:TABLE_ROWS, 0:per] = energies[...]
    for q in range(COLS):
        grids(q, 0).wait()
    naming.wait()


def split(x):
    high = x.astype(BF16)
    return high, (x - high.astype(F32)).astype(BF16)


def pick(values, chosen):
    both = jnp.concatenate(split(values), axis=1)
    return jnp.dot(both, jnp.concatenate([chosen, chosen], axis=0), preferred_element_type=F32)


def ones_where(condition):
    return jnp.where(condition, 1.0, 0.0).astype(BF16)


def repeat_rows(x, count):
    rows, lanes = x.shape
    return jnp.broadcast_to(x[:, None, :], (rows, count, lanes)).reshape(rows * count, lanes)


def sigma_kernel(
    sources_live, pay, table_0, table_1, table_2, table_3, spectator, vectors, out,
    held, matrix, folded, summed, modal_j, modal_k, level, spread, used, order, in_sem, out_sem,
):
    blocks = held.shape[0]
    sources, live = sources_live.at[0], sources_live.at[1]

    def load(b):
        return pltpu.make_async_copy(vectors.at[b], held.at[b], in_sem.at[b])

    def store(b):
        return pltpu.make_async_copy(held.at[b], out.at[b], out_sem)

    for s in range(COLS):
        used[s] = 0

    @pl.loop(0, blocks)
    def _(b):
        used[sources[b]] = 1
        load(b).start()

    me = lax.axis_index("trip")


    def owner_of(slot):
        return (me ^ (slot & 3) ^ jnp.where((slot & 4) > 0, 6, 0)).astype(F32)

    owner = owner_of(iota((1, HALF), 1) // MODAL_ROWS)
    within = (iota((1, HALF), 1) % MODAL_ROWS).astype(F32)
    named = pay[:, G, :]
    owners = [named[:, n : n + 1] for n in range(3)]
    places = [named[:, n + 3 : n + 4] for n in range(3)]
    chosen = jnp.concatenate(
        [ones_where((owners[n] == owner) & (places[n] == within)) for n in range(3)], axis=0
    )
    tables = [
        table[n : n + TABLE_ROWS, :]
        for table in (table_0, table_1, table_2, table_3)
        for n in (0, TABLE_ROWS)
    ]
    modals = jnp.concatenate([table[0:MODAL_ROWS] for table in tables], axis=0)
    levels = jnp.concatenate([table[MODAL_ROWS:] for table in tables], axis=0)
    levels = jnp.concatenate([levels, jnp.zeros_like(levels)], axis=0)
    high, low = split(modals)
    rows = jnp.dot(chosen, high, preferred_element_type=F32) + jnp.dot(
        chosen, low, preferred_element_type=F32
    )
    own_modal = iota((128, 128), 1) // G == iota((128, 128), 0) % NMOD
    first, second, third = (
        jnp.where(own_modal, repeat_rows(rows[16 * n : 16 * n + 16], NMOD), 0.0)
        for n in range(3)
    )
    by_major = ones_where(iota((128, HALF), 1) // G == iota((128, HALF), 0) % G)
    by_minor = ones_where(iota((128, HALF), 1) % G == iota((128, HALF), 0) % G)
    modal_i = pick(first, by_minor[:, 0:128])
    part = iota((64, 128), 1) // G
    empty = jnp.zeros((128 - 3 * G, HALF), BF16)
    for n in range(COLS):
        mine = modal_i[8 * n : 8 * n + 8]
        high, low = split((mine[:, None, :] * mine[None, :, :]).reshape(64, 128))
        squares = jnp.where(part == 1, low.astype(F32), jnp.where(part < 3, high.astype(F32), 0.0))
        grid_high, grid_low = split(pay[n, 0:G, :])
        grids = jnp.concatenate([grid_high, grid_high, grid_low, empty], axis=0)
        summed[64 * n : 64 * n + 64, :] = jnp.dot(
            squares.astype(BF16), grids, preferred_element_type=F32
        )
    modal_j[...] = pick(second, by_major)
    modal_k[...] = pick(third, by_minor)
    level_high, level_low = split(levels)
    table_levels = jnp.concatenate([level_high, level_low], axis=0)
    lane = iota((1, 128), 1)
    level_owner = jnp.where(lane < 64, owner_of(lane // NMOD), -1.0)
    row, col = iota((128, 128), 0), iota((128, 128), 1)
    parts = []
    for n, digit in enumerate((col % 8, (col // 8) % 8, col % 8)):
        at = ones_where(places[n] == lane.astype(F32))
        found = lax.dot_general(
            at, table_levels, (((1,), (1,)), ((), ())), preferred_element_type=F32
        )
        own = jnp.where(owners[n] == level_owner, found[:, 0:128] + found[:, 128:256], 0.0)
        parts.append(pick(own, ones_where(row % NMOD == digit)))
    rest = parts[1] + parts[2]
    for a in range(NMOD):
        level[:, 128 * a : 128 * a + 128] = rest + parts[0][:, a : a + 1]
    padded = jnp.concatenate([spectator[...], jnp.zeros((blocks, 120), F32)], axis=1)
    spread[...] = pick(padded, ones_where(iota((128, S), 0) == iota((128, S), 1) // NVEC))

    on_left = iota((64, 128), 1) < 64
    on_diagonal = iota((64, 128), 1) % 64 == iota((64, 128), 0)
    combos = [(a, n) for a in range(NMOD) for n in range(a, NMOD)]
    place = {c: 64 * i for i, c in enumerate(combos)}
    place |= {(n, a): at for (a, n), at in place.items()}

    def build(s, spot):
        eight = pl.ds(pl.multiple_of(s * 8, 8), 8)
        pairs = (modal_j[eight, :][:, None, :] * modal_k[eight, :][None, :, :]).reshape(64, HALF)
        half = pairs.astype(BF16)
        weights = jnp.concatenate([half, half], axis=0)
        levels = level[pl.ds(s, 1), :]
        grids = [
            summed[pl.ds(pl.multiple_of(s * 64, 64) + a * NMOD, NMOD), :] for a in range(NMOD)
        ]
        scaled = [(grids[a][n : n + 1] * pairs).astype(BF16) for a, n in combos]
        whole = lax.dot_general(
            jnp.concatenate(scaled, axis=0),
            weights,
            (((1,), (1,)), ((), ())),
            preferred_element_type=F32,
        )
        for i, (a, n) in enumerate(combos):
            one = whole[64 * i : 64 * i + 64, :]
            if a == n:
                one = one + jnp.where(on_diagonal, levels[:, 128 * a : 128 * a + 128], 0.0)
            folded[spot, 64 * i : 64 * i + 64, :] = one.astype(BF16)

    def spread_out(s, spot):
        for a in range(NMOD):
            for j in range(NMOD // 2):
                even, odd = place[a, 2 * j], place[a, 2 * j + 1]
                matrix[s, j, 64 * a : 64 * a + 64, :] = jnp.where(
                    on_left, folded[spot, even : even + 64, :], folded[spot, odd : odd + 64, :]
                )

    count = jnp.int32(0)
    for s in range(COLS):
        order[count] = s
        count = count + used[s]
    order[count] = order[jnp.maximum(count - 1, 0)]

    @pl.loop(0, (count + 1) // 2)
    def _(step):
        here, there = order[2 * step], order[2 * step + 1]
        build(here, 0)
        build(there, 1)
        spread_out(here, 0)
        spread_out(there, 1)

    def product(b):
        whole = jnp.concatenate([matrix[sources[b], n] for n in range(4)], axis=1)
        return jnp.dot(whole, held[b], preferred_element_type=F32)

    def finish(b, block):
        scale = spread[pl.ds(b, 1), :]
        kept = ones_where(iota((1, S), 1) < live[b] * NVEC)
        held[b] = (block + scale * held[b].astype(F32)).astype(BF16) * kept
        store(b).start()

    @pl.loop(0, blocks // UNROLL)
    def _(step):
        first = step * UNROLL
        for n in range(UNROLL):
            load(first + n).wait()

        block = product(first)
        for n in range(UNROLL):
            later = product(first + n + 1) if n + 1 < UNROLL else None
            finish(first + n, block)
            block = later

    pltpu.make_async_copy(held, out, out_sem).wait()


def late_call(sources, live, received, tables, spectator, vectors):
    vmem, smem = pl.BlockSpec(memory_space=pltpu.VMEM), pl.BlockSpec(memory_space=pltpu.SMEM)
    anywhere = pl.BlockSpec(memory_space=pl.ANY)
    blocks = vectors.shape[0]
    return pl.pallas_call(
        sigma_kernel,
        out_shape=jax.ShapeDtypeStruct(vectors.shape, BF16),
        in_specs=[smem, vmem, vmem, vmem, vmem, vmem, vmem, anywhere],
        out_specs=anywhere,
        scratch_shapes=[
            pltpu.VMEM((blocks, S, S), BF16),
            pltpu.VMEM((COLS, 4, S, 128), BF16),
            pltpu.VMEM((2, 36 * 64, 128), BF16),
            pltpu.VMEM((COLS * 64, HALF), F32),
            pltpu.VMEM((128, HALF), F32),
            pltpu.VMEM((128, HALF), F32),
            pltpu.VMEM((COLS, 2 * S), F32),
            pltpu.VMEM((blocks, S), F32),
            pltpu.SMEM((COLS,), jnp.int32),
            pltpu.SMEM((COLS + 1,), jnp.int32),
            pltpu.SemaphoreType.DMA((blocks,)),
            pltpu.SemaphoreType.DMA,
        ],
        compiler_params=pltpu.CompilerParams(vmem_limit_bytes=48 * 2**20),
        cost_estimate=pl.CostEstimate(
            flops=2 * (blocks + COLS) * S**3, bytes_accessed=4 * blocks * S * S, transcendentals=0
        ),
    )(jnp.stack([sources, live]), received, *tables, spectator, vectors)


def on_device(
    pes_grids,
    modals,
    energies,
    triple_modes,
    routing,
    block_source,
    live_rows,
    trial_vectors,
    spectator_energy,
):
    vmem, smem = pl.BlockSpec(memory_space=pltpu.VMEM), pl.BlockSpec(memory_space=pltpu.SMEM)
    pay, table = pl.pallas_call(
        pack_kernel,
        out_shape=(
            jax.ShapeDtypeStruct((COLS, PAY_ROWS, HALF), F32),
            jax.ShapeDtypeStruct((TABLE_ROWS, 128), F32),
        ),
        in_specs=[smem, smem, pl.BlockSpec(memory_space=pl.ANY), vmem, vmem],
        out_specs=(pl.BlockSpec(memory_space=pl.ANY), vmem),
        scratch_shapes=[
            pltpu.VMEM((COLS, 8, HALF), F32),
            pltpu.SemaphoreType.DMA((COLS + 1,)),
        ],
    )(routing.reshape(COLS), triple_modes, pes_grids, modals, energies.T)
    received = lax.all_to_all(pay, "exc", split_axis=0, concat_axis=0, tiled=True)

    def swap(x, step):
        return lax.ppermute(x, "trip", [(n, n ^ step) for n in range(TRIPS)])

    both = jnp.concatenate([table, swap(table, 1)], axis=0)
    near, far = swap(both, 2), swap(both, 6)
    tables = (both, near, far, swap(both, 4))
    return late_call(
        block_source, live_rows, received, tables, spectator_energy, trial_vectors
    )


def solution(mesh):
    in_specs = (
        P(("trip", "exc"), None, None),
        P("trip", None),
        P("trip", None),
        P(("trip", "exc"), None),
        P("trip", None, "exc"),
        P(("trip", "exc")),
        P(("trip", "exc")),
        P(("trip", "exc"), None, None),
        P(("trip", "exc"), None),
    )
    out_specs = P(("trip", "exc"), None, None)
    return jax.shard_map(
        on_device, mesh=mesh, in_specs=in_specs, out_specs=out_specs, check_vma=False
    )
```
